256 devices in a mesh: pts: 64 (over z, y, core), head: 4 (over x).
Axes of the slice: x: 4, y: 4, z: 8, core: 2. Of those that a mesh axis runs over, the one named last changes fastest.
Arguments:
- cloud_samples: bfloat16 [655360, 256], P('pts'), may hold values from -6 to 6
- incoming_cotangent: bfloat16 [655360, 256], P('pts'), may hold values from -6 to 6
- entry_mapping_couple: bfloat16 [2, 256, 256], P(None, None, 'head'), may hold values from -0.375 to 0.375
- cluster_mapping_table: bfloat16 [8, 32, 64], P('head'), may hold values from -1 to 1
- warmth_factor: float32 [8], P('head'), may hold values from 0.01 to 1
- attention_maps_table: bfloat16 [3, 32, 32], replicated, may hold values from -4 to 4
- exit_mapping_table: bfloat16 [256, 256], P('head'), may hold values from -0.375 to 0.375
Outputs:
- points_grad: bfloat16 [655360, 256], P(('pts', 'head'))
- projin_grad: float32 [2, 256, 256], P(None, None, 'head')
- slices_grad: float32 [8, 32, 64], P('head')
- warmth_derivative: float32 [8], P('head')
- qkv_grad: float32 [3, 32, 32], replicated
- projout_grad: float32 [256, 256], P('head')
The draws below stay inside these ranges and needn't reach their ends.
All inputs are finite; a program needn't handle non-finite values.
Results may differ from the reference program's by a relative error of at most 0.017.
Values may be sent and summed in bfloat16 or wider, within the bound.
No kernel may reach another device: no remote copies, remote signals or barrier semaphores. Data moves between devices by JAX's collectives and lax.ppermute only.
A program may use at most 128 MiB of HBM per device.

```python
import math
import jax
import jax.numpy as jnp
from jax import lax

D = 256
H = 8
DH = 32
G = 64
N = 655360


def draw_cloud_samples(key, part):
    key = jax.random.fold_in(key, 7)
    first = jax.random.fold_in(key, 0)
    values = jax.random.normal(first, (N, D), jnp.float32)
    return jnp.clip(values, -6.0, 6.0).astype(jnp.bfloat16)


def draw_warmth_factor(key, part):
    key = jax.random.fold_in(key, 13)
    values = jnp.exp(jax.random.uniform(key, (H,), jnp.float32, math.log(0.05), 0.0))
    return jnp.clip(values, 0.01, 1.0).astype(jnp.float32)


def draw_attention_maps_table(key, part):
    key = jax.random.fold_in(key, 17)
    values = jax.random.normal(key, (3, DH, DH), jnp.float32) * DH ** (-0.5)
    return jnp.clip(values, -4.0, 4.0).astype(jnp.bfloat16)


def block_levels(stream_key, dims, cuts, smallest, top_value):
    level = 1.0
    for position, blocks in cuts:
        steps = jax.random.uniform(jax.random.fold_in(jax.random.fold_in(stream_key, 6), position), (blocks,), jnp.float32, smallest / len(cuts), top_value / len(cuts))
        level = level * jnp.repeat(jnp.exp(steps), dims[position] // blocks).reshape((-1,) + (1,) * (len(dims) - 1 - position))
    return level


def scatter_about(own_key, dims, width, most, shards=(), kind=jnp.bfloat16):
    values = width * jax.random.normal(own_key, dims, jnp.float32)
    if shards:
        values = values * block_levels(own_key, dims, shards, -0.22, 0.18)
    return jnp.clip(values, -most, most).astype(kind)


def setup_inputs(seed: int = 0) -> dict:
    seeds = jax.random.split(jax.random.key(seed), 8)
    cloud_samples = draw_cloud_samples(jax.random.fold_in(seeds[7], 71), 0)
    incoming_cotangent = scatter_about(seeds[1], (N, D), 1.0, 6.0, ((0, 64),))
    entry_mapping_couple = scatter_about(seeds[2], (2, D, H * DH), D ** -0.5, 0.375, ((2, 4),))
    cluster_mapping_table = scatter_about(seeds[3], (H, DH, G), DH ** -0.5, 1.0, ((0, 4),))
    warmth_factor = draw_warmth_factor(jax.random.fold_in(seeds[7], 71), 0)
    attention_maps_table = draw_attention_maps_table(jax.random.fold_in(seeds[7], 71), 0)
    exit_mapping_table = scatter_about(seeds[6], (H * DH, D), (H * DH) ** -0.5, 0.375, ((0, 4),))
    return {"cloud_samples": cloud_samples, "incoming_cotangent": incoming_cotangent, "entry_mapping_couple": entry_mapping_couple, "cluster_mapping_table": cluster_mapping_table, "warmth_factor": warmth_factor, "attention_maps_table": attention_maps_table, "exit_mapping_table": exit_mapping_table}


epsilon = 1e-5
maximal_accuracy = lax.Precision.HIGHEST


def token_attention(tokens, attention_maps_table):
    weights = attention_maps_table.astype(jnp.float32)
    score_scale = tokens.shape[-1] ** -0.5
    queries = jnp.einsum("hgd,de->hge", tokens, weights[0], precision=maximal_accuracy)
    keys_all = jnp.einsum("hgd,de->hge", tokens, weights[1], precision=maximal_accuracy)
    values = jnp.einsum("hgd,de->hge", tokens, weights[2], precision=maximal_accuracy)
    scores = jnp.einsum("hgd,hkd->hgk", queries, keys_all, precision=maximal_accuracy) * score_scale
    attend = jax.nn.softmax(scores, axis=-1)
    mixed_tokens = jnp.einsum("hgk,hkd->hgd", attend, values, precision=maximal_accuracy)
    return queries, keys_all, values, attend, mixed_tokens


def token_backward(tokens, attention_maps_table, saved_state, grad_mixed):
    weights = attention_maps_table.astype(jnp.float32)
    score_scale = tokens.shape[-1] ** -0.5
    queries, keys_all, values, attend, mixed_tokens = saved_state
    grad_attend = jnp.einsum("hgd,hkd->hgk", grad_mixed, values, precision=maximal_accuracy)
    grad_scores = attend * (grad_attend - jnp.sum(attend * grad_attend, axis=-1, keepdims=True))
    grad_query = jnp.einsum("hgk,hkd->hgd", grad_scores, keys_all, precision=maximal_accuracy) * score_scale
    grad_keys = jnp.einsum("hgk,hgd->hkd", grad_scores, queries, precision=maximal_accuracy) * score_scale
    grad_values = jnp.einsum("hgk,hgd->hkd", attend, grad_mixed, precision=maximal_accuracy)
    grad_tokens = jnp.einsum("hge,de->hgd", grad_query, weights[0], precision=maximal_accuracy)
    grad_tokens = grad_tokens + jnp.einsum("hge,de->hgd", grad_keys, weights[1], precision=maximal_accuracy)
    grad_tokens = grad_tokens + jnp.einsum("hge,de->hgd", grad_values, weights[2], precision=maximal_accuracy)
    grad_weights = jnp.stack([
        jnp.einsum("hgd,hge->de", tokens, grad_query, precision=maximal_accuracy),
        jnp.einsum("hgd,hge->de", tokens, grad_keys, precision=maximal_accuracy),
        jnp.einsum("hgd,hge->de", tokens, grad_values, precision=maximal_accuracy)])
    return grad_tokens, grad_weights


def reference(cloud_samples, incoming_cotangent, entry_mapping_couple, cluster_mapping_table, warmth_factor, attention_maps_table, exit_mapping_table):
    upstream_wide = incoming_cotangent.astype(jnp.float32)

    def one_head(carry, attender_index):
        grad_rows, grad_qkv = carry
        begin_col = (attender_index * DH).astype(jnp.int32)
        key_cols = lax.dynamic_slice_in_dim(entry_mapping_couple[0], begin_col, DH, 1)
        feat_cols = lax.dynamic_slice_in_dim(entry_mapping_couple[1], begin_col, DH, 1)
        out_rows = lax.dynamic_slice_in_dim(exit_mapping_table, begin_col, DH, 0)
        cluster_table = lax.dynamic_index_in_dim(cluster_mapping_table, attender_index, 0, keepdims=False).astype(jnp.float32)
        normalizer_warmth = lax.dynamic_index_in_dim(warmth_factor, attender_index, 0, keepdims=False)
        labelled_tokens = jnp.dot(cloud_samples, key_cols, preferred_element_type=jnp.float32)
        features = jnp.dot(cloud_samples, feat_cols, preferred_element_type=jnp.float32)
        cluster_score_lines = jnp.dot(labelled_tokens, cluster_table, precision=maximal_accuracy) / normalizer_warmth
        slice_weight = jax.nn.softmax(cluster_score_lines, axis=-1)
        numer = jnp.dot(slice_weight.T, features, precision=maximal_accuracy)
        denom = jnp.sum(slice_weight, axis=0)
        tokens = numer / (denom + epsilon)[:, None]
        saved_state = token_attention(tokens[None], attention_maps_table)
        mixed_tokens = saved_state[4][0]
        grad_slot = jnp.dot(incoming_cotangent, out_rows.T, preferred_element_type=jnp.float32)
        spread_rows = jnp.dot(slice_weight, mixed_tokens, precision=maximal_accuracy)
        out_grad = jnp.dot(spread_rows.T, upstream_wide, precision=maximal_accuracy)
        grad_mixed = jnp.dot(slice_weight.T, grad_slot, precision=maximal_accuracy)
        grad_tokens, qkv_part = token_backward(tokens[None], attention_maps_table, saved_state, grad_mixed[None])
        grad_tokens = grad_tokens[0]
        shifted_den = denom + epsilon
        grad_numer = grad_tokens / shifted_den[:, None]
        grad_denom = -jnp.sum(grad_tokens * tokens, axis=-1) / shifted_den
        grad_weight = jnp.dot(grad_slot, mixed_tokens.T, precision=maximal_accuracy)
        grad_weight = grad_weight + jnp.dot(features, grad_numer.T, precision=maximal_accuracy) + grad_denom[None, :]
        raw_score_derivative = slice_weight * (grad_weight - jnp.sum(slice_weight * grad_weight, axis=-1, keepdims=True))
        derivative_of_labelled = jnp.dot(raw_score_derivative, cluster_table.T, precision=maximal_accuracy) / normalizer_warmth
        grad_feat = jnp.dot(slice_weight, grad_numer, precision=maximal_accuracy)
        cluster_derivative = jnp.dot(labelled_tokens.T, raw_score_derivative, precision=maximal_accuracy) / normalizer_warmth
        warmth_derivative = -jnp.sum(raw_score_derivative * cluster_score_lines) / normalizer_warmth
        key_round = derivative_of_labelled.astype(jnp.bfloat16)
        feat_round = grad_feat.astype(jnp.bfloat16)
        grad_rows = grad_rows + jnp.dot(key_round, key_cols.T, preferred_element_type=jnp.float32)
        grad_rows = grad_rows + jnp.dot(feat_round, feat_cols.T, preferred_element_type=jnp.float32)
        contract = (((0,), (0,)), ((), ()))
        input_key = lax.dot_general(cloud_samples, key_round, contract, preferred_element_type=jnp.float32)
        input_feat = lax.dot_general(cloud_samples, feat_round, contract, preferred_element_type=jnp.float32)
        outputs = (jnp.stack([input_key, input_feat]), cluster_derivative, warmth_derivative, out_grad)
        return (grad_rows, grad_qkv + qkv_part), outputs

    start_state = (jnp.zeros((N, D), jnp.float32), jnp.zeros((3, DH, DH), jnp.float32))
    finals, stacked = lax.scan(one_head, start_state, jnp.arange(H, dtype=jnp.int32))
    grad_rows, qkv_grad = finals
    input_stack, slices_grad, warmth_derivative, out_stack = stacked
    projin_grad = input_stack.transpose(1, 2, 0, 3).reshape(2, D, H * DH)
    projout_grad = out_stack.reshape(H * DH, D)
    return (grad_rows.astype(jnp.bfloat16), projin_grad, slices_grad, warmth_derivative, qkv_grad, projout_grad)
```

```python
import jax
import jax.numpy as jnp
from jax import lax
from jax.sharding import Mesh
from jax.sharding import PartitionSpec as P

epsilon = 1e-05
maximal_accuracy = lax.Precision.HIGHEST


def swap_axis(values, axis, offset):
    size = lax.axis_size(axis)
    return lax.ppermute(values, axis, [(i, i ^ offset) for i in range(size)])


def spread(values, axes, count):
    return lax.all_to_all(
        jnp.broadcast_to(values[None], (count, *values.shape)), axes, 0, 0, tiled=True
    )


def sum_four(values, axis):
    one, two, three = (swap_axis(values, axis, k) for k in (1, 2, 3))
    return (values + one) + (two + three)


def sum_small(values):
    values = values + swap_axis(values, "core", 1)
    values = sum_four(values, "y")
    return spread(values, "z", lax.axis_size("z")).sum(0)


def sum_large(values):
    rows = values.shape[0]
    plane = lax.axis_size("y") * lax.axis_size("core")
    part = values.astype(jnp.bfloat16).reshape(plane, rows // plane, 128)
    part = lax.all_to_all(part, ("y", "core"), 0, 0, tiled=True).astype(jnp.float32).sum(0)
    part = spread(part.astype(jnp.bfloat16), "z", lax.axis_size("z")).astype(jnp.float32).sum(0)
    return spread(part.astype(jnp.bfloat16), ("y", "core"), plane).astype(jnp.float32).reshape(rows, 128)


def flat_sum(arrays, adder, rows):
    flat = jnp.concatenate([a.reshape(-1) for a in arrays])
    flat = jnp.pad(flat, (0, rows * 128 - flat.shape[0])).reshape(rows, 128)
    total = adder(flat).reshape(-1)
    out, at = [], 0
    for a in arrays:
        out.append(total[at : at + a.size].reshape(a.shape))
        at += a.size
    return out


def token_attention(tokens, attention_maps_table):
    weights = attention_maps_table.astype(jnp.float32)
    score_scale = tokens.shape[-1] ** (-0.5)
    queries = jnp.einsum("hgd,de->hge", tokens, weights[0], precision=maximal_accuracy)
    keys_all = jnp.einsum("hgd,de->hge", tokens, weights[1], precision=maximal_accuracy)
    values = jnp.einsum("hgd,de->hge", tokens, weights[2], precision=maximal_accuracy)
    scores = jnp.einsum("hgd,hkd->hgk", queries, keys_all, precision=maximal_accuracy) * score_scale
    attend = jax.nn.softmax(scores, axis=-1)
    mixed_tokens = jnp.einsum("hgk,hkd->hgd", attend, values, precision=maximal_accuracy)
    return (queries, keys_all, values, attend, mixed_tokens)


def token_backward(tokens, attention_maps_table, saved_state, grad_mixed):
    weights = attention_maps_table.astype(jnp.float32)
    score_scale = tokens.shape[-1] ** (-0.5)
    queries, keys_all, values, attend, mixed_tokens = saved_state
    grad_attend = jnp.einsum("hgd,hkd->hgk", grad_mixed, values, precision=maximal_accuracy)
    grad_scores = attend * (grad_attend - jnp.sum(attend * grad_attend, axis=-1, keepdims=True))
    grad_query = (
        jnp.einsum("hgk,hkd->hgd", grad_scores, keys_all, precision=maximal_accuracy) * score_scale
    )
    grad_keys = (
        jnp.einsum("hgk,hgd->hkd", grad_scores, queries, precision=maximal_accuracy) * score_scale
    )
    grad_values = jnp.einsum("hgk,hgd->hkd", attend, grad_mixed, precision=maximal_accuracy)
    grad_tokens = jnp.einsum("hge,de->hgd", grad_query, weights[0], precision=maximal_accuracy)
    grad_tokens = grad_tokens + jnp.einsum(
        "hge,de->hgd", grad_keys, weights[1], precision=maximal_accuracy
    )
    grad_tokens = grad_tokens + jnp.einsum(
        "hge,de->hgd", grad_values, weights[2], precision=maximal_accuracy
    )
    grad_weights = jnp.stack(
        [
            jnp.einsum("hgd,hge->de", tokens, grad_query, precision=maximal_accuracy),
            jnp.einsum("hgd,hge->de", tokens, grad_keys, precision=maximal_accuracy),
            jnp.einsum("hgd,hge->de", tokens, grad_values, precision=maximal_accuracy),
        ]
    )
    return (grad_tokens, grad_weights)


def output_part(slice_weight, mixed_tokens, incoming_cotangent, row_count, inner_width):
    spread_rows = jnp.einsum("phg,hgd->phd", slice_weight, mixed_tokens, precision=maximal_accuracy)
    spread_rows = spread_rows.reshape(row_count, inner_width)
    return jnp.einsum(
        "pi,pe->ie",
        spread_rows,
        incoming_cotangent,
        precision=maximal_accuracy,
        preferred_element_type=jnp.float32,
    )


def local(
    cloud_samples,
    incoming_cotangent,
    entry_mapping_couple,
    cluster_mapping_table,
    warmth_factor,
    attention_maps_table,
    exit_mapping_table,
):
    row_count = cloud_samples.shape[0]
    width = cloud_samples.shape[1]
    local_heads, head_dim, slice_count = cluster_mapping_table.shape
    inner_width = local_heads * head_dim
    head_count = lax.axis_size("x")
    col_stack = jnp.concatenate([entry_mapping_couple[0], entry_mapping_couple[1]], axis=1)
    projected = jnp.dot(cloud_samples, col_stack, preferred_element_type=jnp.float32)
    labelled_tokens = projected[:, :inner_width].reshape(row_count, local_heads, head_dim)
    features = projected[:, inner_width:].reshape(row_count, local_heads, head_dim)
    slice_mats = cluster_mapping_table.astype(jnp.float32)
    cluster_score_lines = (
        jnp.einsum("phd,hdg->phg", labelled_tokens, slice_mats, precision=maximal_accuracy)
        / warmth_factor[None, :, None]
    )
    slice_weight = jax.nn.softmax(cluster_score_lines, axis=-1)
    numer_part = jnp.einsum("phg,phd->hgd", slice_weight, features, precision=maximal_accuracy)
    denom_part = jnp.sum(slice_weight, axis=0)
    grad_slot = jnp.dot(
        incoming_cotangent, exit_mapping_table.T, preferred_element_type=jnp.float32
    )
    grad_slot = grad_slot.reshape(row_count, local_heads, head_dim)
    mixed_part = jnp.einsum("phg,phd->hgd", slice_weight, grad_slot, precision=maximal_accuracy)
    numer, denom, grad_mixed = flat_sum([numer_part, denom_part, mixed_part], sum_small, 72)
    shifted_den = denom + epsilon
    tokens = numer / shifted_den[..., None]
    saved_state = token_attention(tokens, attention_maps_table)
    mixed_tokens = saved_state[4]
    grad_tokens, qkv_part = token_backward(tokens, attention_maps_table, saved_state, grad_mixed)
    qkv_grad = sum_four(qkv_part, "x")
    grad_numer = grad_tokens / shifted_den[..., None]
    grad_denom = -jnp.sum(grad_tokens * tokens, axis=-1) / shifted_den
    grad_weight = jnp.einsum("phd,hgd->phg", grad_slot, mixed_tokens, precision=maximal_accuracy)
    grad_weight = grad_weight + jnp.einsum(
        "phd,hgd->phg", features, grad_numer, precision=maximal_accuracy
    )
    grad_weight = grad_weight + grad_denom[None, :, :]
    raw_score_derivative = slice_weight * (
        grad_weight - jnp.sum(slice_weight * grad_weight, axis=-1, keepdims=True)
    )
    derivative_of_labelled = (
        jnp.einsum("phg,hdg->phd", raw_score_derivative, slice_mats, precision=maximal_accuracy)
        / warmth_factor[None, :, None]
    )
    grad_feat = jnp.einsum("phg,hgd->phd", slice_weight, grad_numer, precision=maximal_accuracy)
    cluster_portion = (
        jnp.einsum(
            "phd,phg->hdg", labelled_tokens, raw_score_derivative, precision=maximal_accuracy
        )
        / warmth_factor[:, None, None]
    )
    warmth_portion = (
        -jnp.sum(raw_score_derivative * cluster_score_lines, axis=(0, 2)) / warmth_factor
    )
    grad_cols = jnp.concatenate(
        [
            derivative_of_labelled.reshape(row_count, inner_width),
            grad_feat.reshape(row_count, inner_width),
        ],
        axis=1,
    ).astype(jnp.bfloat16)
    contract = (((0,), (0,)), ((), ()))
    entering_portion = lax.dot_general(
        cloud_samples, grad_cols, contract, preferred_element_type=jnp.float32
    )
    entering_portion = entering_portion.reshape(width, 2, inner_width).transpose(1, 0, 2)
    result_nearby = output_part(
        slice_weight, mixed_tokens, incoming_cotangent, row_count, inner_width
    )
    projin_grad, slices_grad, warmth_derivative, projout_grad = flat_sum(
        [entering_portion, cluster_portion, warmth_portion, result_nearby], sum_large, 512
    )
    all_weights = lax.all_gather(entry_mapping_couple, "x", axis=2, tiled=True)
    received = lax.all_to_all(grad_cols, "x", split_axis=0, concat_axis=1, tiled=True)
    blocks = received.reshape(row_count // head_count, head_count, 2, inner_width)
    arranged = all_weights.reshape(2, width, head_count, inner_width)
    points_grad = jnp.einsum(
        "pcsk,sdck->pd", blocks, arranged, preferred_element_type=jnp.float32
    ).astype(jnp.bfloat16)
    return (points_grad, projin_grad, slices_grad, warmth_derivative, qkv_grad, projout_grad)


def solution(mesh):
    grid = Mesh(mesh.devices.reshape(8, 4, 2, 4), ("z", "y", "core", "x"))
    points = ("z", "y", "core")
    return jax.shard_map(
        local,
        mesh=grid,
        in_specs=(
            P(points, None),
            P(points, None),
            P(None, None, "x"),
            P("x", None, None),
            P("x"),
            P(),
            P("x", None),
        ),
        out_specs=(
            P((*points, "x"), None),
            P(None, None, "x"),
            P("x", None, None),
            P("x"),
            P(),
            P("x", None),
        ),
        check_vma=False,
    )
```
